256 devices in a mesh: scen: 16 (over z_lo, x), row: 2 (over core), col: 8 (over y, z_hi).
Axes of the slice: x: 4, y: 4, z: 8 (z_hi: 2, z_lo: 4; z = z_hi * 4 + z_lo), core: 2. Of those that a mesh axis runs over, the one named last changes fastest.
Arguments:
- kkt: float32 [48, 768, 768], P('scen', ('row', 'col')), as said below
- border: float32 [48, 768, 4096], P('scen', None, ('row', 'col')), may hold values from -0.15625 to 0.15625
- first_diag: float32 [4096], P('scen'), may hold values from 0.5 to 1.5
- assignment: int32 [48], P('scen'), may hold values from 0 to 47, as said below
- panel: int32 [8], replicated, may hold values from 0 to 7, each once
Outputs:
- schur: float32 [4096, 4096], P('scen', ('row', 'col'))
- panel_factor: float32 [4096, 512], P('scen', ('row', 'col'))
The draws below stay inside these ranges and needn't reach their ends.
Inputs may be any that keep to these rules, and one draw needn't show every extreme that they name: assignment is a permutation; with k = d * 3 + j (0 <= j < 3), assignment[k] is either k or (d XOR 1) * 3 + j, and the two scenarios of such a pair are either both fixed or swapped. panel is a permutation. Each kkt block is symmetric positive definite; after scaling by its diagonal, the off-diagonal part has spectral norm about one half.
All inputs are finite; a program needn't handle non-finite values.
Results may differ from the reference program's by a relative error of at most 0.00015.
Values sent between devices are 32-bit elements; how exact they have to be, the bound alone decides.
No kernel may reach another device: no remote copies, remote signals or barrier semaphores. Data moves between devices by JAX's collectives and lax.ppermute only.
A program may use at most 128 MiB of HBM per device.

```python
import math
import jax
import jax.numpy as jnp
from jax import lax

NK = 768
NF = 4096
PW = 512
NEWTON = 3
S_DEV = 3
NSCEN = 48


def draw_kkt(key, part):
    first_key, second_key, third_key = jax.random.split(jax.random.fold_in(key, 11), 3)
    entry_scale = jnp.exp(jax.random.uniform(first_key, (NSCEN, NK), minval=math.log(0.5), maxval=math.log(4.0)))
    scen_scale = jnp.exp(jax.random.uniform(third_key, (NSCEN, 1), minval=math.log(0.5), maxval=math.log(4.0)))
    scales = entry_scale * scen_scale
    noise = jax.random.normal(second_key, (NSCEN, NK, NK))
    paired = (noise + jnp.swapaxes(noise, 1, 2)) * (0.25 / math.sqrt(2.0 * NK))
    paired = paired * (1.0 - jnp.eye(NK, dtype=jnp.float32))[None]
    roots = jnp.sqrt(scales)
    blocks = roots[:, :, None] * paired * roots[:, None, :]
    blocks = blocks + jnp.eye(NK, dtype=jnp.float32)[None] * scales[:, :, None]
    return blocks.astype(jnp.float32)


def draw_assignment(key, part):
    groups = NSCEN // S_DEV
    flips = jax.random.randint(jax.random.fold_in(key, 23), (groups // 2, S_DEV), 0, 2)
    flips = jnp.repeat(flips, 2, axis=0)
    device_ids = jnp.arange(groups, dtype=jnp.int32)[:, None]
    slot_ids = jnp.arange(S_DEV, dtype=jnp.int32)[None, :]
    own = device_ids * S_DEV + slot_ids
    other = (device_ids + 1 - 2 * (device_ids % 2)) * S_DEV + slot_ids
    chosen = jnp.where(flips == 1, other, own)
    return chosen.reshape(-1).astype(jnp.int32)


def block_levels(key, extent, cuts, low, high):
    loudness, own = 1.0, jax.random.fold_in(key, 6)
    for position, parts in cuts:
        draws = jnp.exp(jax.random.uniform(jax.random.fold_in(own, position), (parts,), jnp.float32, low / len(cuts), high / len(cuts)))
        loudness = loudness * jnp.repeat(draws, extent[position] // parts).reshape([-1 if axis == position else 1 for axis in range(len(extent))])
    return loudness


def bell_draw(stream_key, dims, scale, most, shards=(), kind=jnp.bfloat16):
    loudness = block_levels(stream_key, dims, shards, -0.22, 0.18) if shards else 1.0
    array = jax.random.normal(stream_key, dims, jnp.float32) * scale * loudness
    return jnp.minimum(jnp.maximum(array, -most), most).astype(kind)


def setup_inputs(seed: int = 0) -> dict:
    keys = jax.random.split(jax.random.key(seed), 6)
    kkt = draw_kkt(jax.random.fold_in(keys[5], 71), 0)
    border = bell_draw(keys[1], (NSCEN, NK, NF), (2.0 * (NK * NSCEN) ** -0.5), 0.15625, ((0, 16), (2, 16)), jnp.float32)
    first_diag = jnp.clip(0.5 + 1.0 * jax.random.uniform(keys[2], (NF,), jnp.float32) ** block_levels(keys[2], (NF,), ((0, 16),), -0.2, 0.2), 0.5, 1.5)
    assignment = draw_assignment(jax.random.fold_in(keys[5], 71), 0)
    panel = jax.random.permutation(keys[4], NF // PW).astype(jnp.int32)
    return {"kkt": kkt, "border": border, "first_diag": first_diag, "assignment": assignment, "panel": panel}


HIGH = lax.Precision.HIGHEST

def invert(kkt_block):
    inv_diag = 1.0 / jnp.diagonal(kkt_block)
    approx = jnp.diag(inv_diag)
    for step in range(NEWTON):
        left = jnp.dot(approx.astype(jnp.float32), kkt_block.astype(jnp.float32), precision=HIGH, preferred_element_type=jnp.float32)
        approx = 2.0 * approx - jnp.dot(left.astype(jnp.float32), approx.astype(jnp.float32), precision=HIGH, preferred_element_type=jnp.float32)
    return approx

def reference(kkt, border, first_diag, assignment, panel):
    start_schur = jnp.diag(first_diag)

    def add_scenario(index, schur):
        block = lax.dynamic_index_in_dim(kkt, index, 0, keepdims=False)
        approx = invert(block)
        chosen = lax.dynamic_index_in_dim(border, assignment[index], 0, keepdims=False)
        solved = jnp.dot(approx.astype(jnp.float32), chosen.astype(jnp.float32), precision=HIGH, preferred_element_type=jnp.float32)
        return schur + lax.dot_general(chosen.astype(jnp.float32), solved.astype(jnp.float32), (((0,), (0,)), ((), ())), precision=HIGH, preferred_element_type=jnp.float32)
    schur = lax.fori_loop(0, NSCEN, add_scenario, start_schur)
    start = panel[0] * PW
    columns = lax.dynamic_slice_in_dim(schur, start, PW, 1)
    block = lax.dynamic_slice_in_dim(columns, start, PW, 0)
    symmetric = 0.5 * (block + block.T)
    lower_factor = jnp.linalg.cholesky(symmetric)
    factor = lax.linalg.triangular_solve(lower_factor, columns, left_side=False, lower=True, transpose_a=True)
    return (schur, factor)
```

```python
import jax
import jax.numpy as jnp
from jax import lax
from jax.sharding import PartitionSpec as P

AXES = ("scen", "row", "col")
HIGH = lax.Precision.HIGH
HIGHEST = lax.Precision.HIGHEST
HORNER = 7


def place(device):
    scen, rest = divmod(device, 16)
    r, c = divmod(rest, 8)
    return (scen // 4, scen % 4, r, c // 2, c % 2)


def number(zl, x, r, y, h):
    return ((zl % 4) * 4 + x % 4) * 16 + (r % 2) * 8 + (y % 4) * 2 + h % 2


def block_of(r, y, h):
    return (r % 2) * 8 + (y % 4) * 2 + h % 2


def send(value, where):
    pairs = []
    for device in range(256):
        target = where(*place(device))
        if target is not None:
            pairs.append((device, target))
    return lax.ppermute(value, AXES, pairs)


def to_core(zl, x, r, y, h):
    return number(zl, x, r + 1, y, h)


def to_far(zl, x, r, y, h):
    return number(zl, x, r, y, h + 1)


def to_y(step):
    return lambda zl, x, r, y, h: number(zl, x, r, y + step, h)


def to_x(step):
    return lambda zl, x, r, y, h: number(zl, x + step, r, y, h)


def to_z(step):
    return lambda zl, x, r, y, h: number(zl + step, x, r, y, h)


def to_pair(zl, x, r, y, h):
    return number(zl, x ^ 1, r, y, h)


def pick(array, index, axis=0):
    return lax.dynamic_index_in_dim(array, index, axis, keepdims=False)


def final_target(step):
    def where(zl, x, r, y, h):
        i = block_of
        f, e = divmod(zl, 2)
        t = (x - step) % 4
        if t < 3:
            row, col = i(r, y + t, h ^ f), i(r ^ e, y, h)
        else:
            col, row = i(r, y + 1, h ^ f), i(r ^ e, y, h)
        return row * 16 + col

    return where


def mirror_target(step):
    def where(zl, x, r, y, h):
        if x != step:
            return None
        f, e = divmod(zl, 2)
        col, row = block_of(r, y + 2, h ^ f), block_of(r ^ e, y, h)
        return row * 16 + col

    return where


def contract(left, right):
    return lax.dot_general(
        left, right, (((0,), (0,)), ((), ())), precision=HIGH, preferred_element_type=jnp.float32
    )


def contract_all(left, right):
    return sum(contract(left[slot], right[slot]) for slot in range(left.shape[0]))


def reduce_pieces(parts, axis_index, step_of):
    total = pick(parts, axis_index)
    for step in (1, 2, 3):
        total = total + send(pick(parts, (axis_index + step) % 4), step_of(step))
    return total


def gather_pieces(piece, axis_index, step_of):
    got = [piece] + [send(piece, step_of(step)) for step in (1, 2, 3)]
    ring = jnp.stack([got[0], got[3], got[2], got[1]])
    return lax.dynamic_slice_in_dim(jnp.concatenate([ring, ring]), (4 - axis_index) % 4, 4, 0)


def gather_kkt(rows, x, r, y, h):
    far = send(rows, to_far)
    slots, count, order = rows.shape

    def around(piece):
        up = send(piece, to_y(1))
        down = send(piece, to_y(-1))
        half = count // 2
        across = jnp.concatenate(
            [send(up[:, :half], to_y(1)), send(down[:, half:], to_y(-1))], axis=1
        )
        ring = jnp.stack([piece, down, across, up], axis=1)
        return lax.dynamic_slice_in_dim(
            jnp.concatenate([ring, ring], axis=1), (4 - y) % 4, 4, 1
        )

    own, other = around(rows), around(far)
    both = jnp.where(h == 0, jnp.stack([own, other], 2), jnp.stack([other, own], 2))
    core = send(both, to_core)
    everything = jnp.where(r == 0, jnp.stack([both, core], 1), jnp.stack([core, both], 1))
    return everything.reshape(slots, 16 * count, order)


def solve(kkt_full, border):
    inv_diag = (1.0 / jnp.diagonal(kkt_full, axis1=1, axis2=2))[:, :, None]
    solved = inv_diag * border
    for step in range(HORNER):
        product = lax.dot_general(
            kkt_full, solved, (((2,), (1,)), ((0,), (0,))), precision=HIGH,
            preferred_element_type=jnp.float32,
        )
        solved = solved + inv_diag * (border - product)
    return solved


def body(kkt, border, first_diag, assignment, panel):
    scen_index = lax.axis_index("scen")
    own_index = lax.axis_index(("row", "col"))
    zl, x = scen_index // 4, scen_index % 4
    r, y, h = own_index // 8, (own_index // 2) % 4, own_index % 2
    slots, order, width = border.shape
    quarter = width // 4
    first, last = 2 * h, 2 - 2 * h
    lead = 2 * (y // 2)

    far_first = send(pick(border, last), to_far)
    own_one = send(border, to_y(-1))
    own_two = send(send(pick(border, 2 - lead), to_y(1)), to_y(1))

    swapped = send(kkt, to_pair)
    ids = scen_index * slots + jnp.arange(slots, dtype=jnp.int32)
    rows = jnp.where((assignment == ids)[:, None, None], kkt, swapped)
    kkt_full = gather_kkt(rows, x, r, y, h)

    far_mid = send(border[1], to_far)
    far_last = send(pick(border, first), to_far)
    far_first_one = send(far_first, to_y(-1))
    far_two = send(send(far_first, to_y(1)), to_y(1))
    far_mid_one = send(far_mid, to_y(-1))
    shared = jnp.where(y < 2, far_mid, border[1])
    shared_two = send(send(shared, to_y(1)), to_y(1))
    far_last_one = send(far_last, to_y(-1))

    solved = solve(kkt_full, border)
    other = send(solved, to_core)
    wide = jnp.concatenate([solved, other], axis=2)

    eye = jnp.eye(width, dtype=jnp.float32)
    diag = jnp.where(scen_index == own_index, eye * first_diag[:, None], 0.0)

    own_tile = contract_all(border, solved) + diag
    off_tile = contract(far_first, pick(solved, first))
    off_tile = off_tile + jnp.where(h == 0, contract(far_mid, solved[1]), 0.0)
    corner = jnp.stack([own_tile, off_tile]).reshape(2, 4, 4, quarter // 4, width)
    corner = corner.transpose(1, 2, 0, 3, 4)
    corner = reduce_pieces(corner, x, to_x)
    corner = reduce_pieces(corner, zl, to_z)
    corner = jnp.stack([corner, send(corner, to_far)])
    corner = gather_pieces(corner, zl, to_z)
    corner = gather_pieces(corner, x, to_x)
    corner = corner.transpose(2, 3, 0, 1, 4, 5).reshape(2, 2, width, width)
    cross = corner[0, 1] + corner[1, 1].T
    lower_left = jnp.where(h == 0, cross, cross.T)
    upper_left = jnp.where(h == 0, corner[0, 0], corner[1, 0])
    lower_right = jnp.where(h == 0, corner[1, 0], corner[0, 0])
    block = jnp.concatenate(
        [
            jnp.concatenate([upper_left, lower_left.T], axis=1),
            jnp.concatenate([lower_left, lower_right], axis=1),
        ],
        axis=0,
    )
    symmetric = 0.5 * (block + block.T)
    lower_factor = jnp.linalg.cholesky(symmetric)
    inverse = lax.linalg.triangular_solve(
        lower_factor, jnp.eye(2 * width, dtype=jnp.float32), left_side=True, lower=True
    )
    inverse_cols = lax.dynamic_slice_in_dim(inverse, h * width, width, 1)

    wide_first, wide_last = pick(wide, first), pick(wide, last)

    def reduced(own, partner):
        parts = jnp.stack([own, partner]).reshape(2, 4, quarter, 2, width)
        parts = parts.transpose(1, 0, 3, 2, 4).reshape(4, 4, quarter, width)
        return reduce_pieces(reduce_pieces(parts, x, to_x), zl, to_z)

    beside = contract_all(border, other)
    piece_zero = reduced(
        jnp.concatenate([own_tile, beside], axis=1),
        contract(far_first, wide_first) + contract(far_mid, wide[1]) + contract(far_last, wide_last),
    )
    common = contract(shared_two, wide[1])
    piece_two = reduced(
        contract(own_two, pick(wide, lead)) + jnp.where(y < 2, common, 0.0),
        contract(far_two, wide_first) + jnp.where(y < 2, 0.0, common),
    )
    piece_one = reduced(
        contract_all(own_one, wide),
        contract(far_first_one, wide_first)
        + contract(far_mid_one, wide[1])
        + contract(far_last_one, wide_last),
    )
    pieces = jnp.stack([piece_zero, piece_one, piece_two, piece_one])
    got = [send(pick(pieces, (x - step) % 4), final_target(step)) for step in range(4)]
    mirrored = [send(piece_two, mirror_target(step)) for step in range(4)]
    distance = ((scen_index // 2) % 4 - y) % 4
    ring = jnp.concatenate(got + got, axis=0)
    tile = lax.dynamic_slice_in_dim(ring, ((4 - distance) % 4) * quarter, width, 0)
    schur = jnp.where(distance == 3, tile.T, tile) + jnp.concatenate(mirrored, axis=0).T

    share = 2 * width // 16
    term = lax.dot_general(
        inverse_cols, schur, (((1,), (1,)), ((), ())), precision=HIGHEST,
        preferred_element_type=jnp.float32,
    )
    term = jnp.where(own_index // 2 == panel[0], term, 0.0).reshape(16, share, width)
    shares = lax.all_to_all(term, ("row", "col"), 0, 0, tiled=True)
    chosen = lax.dynamic_slice_in_dim(shares, 2 * panel[0], 2, 0)
    return (schur, (chosen[0] + chosen[1]).T)


def solution(mesh):
    in_specs = (
        P("scen", ("row", "col"), None),
        P("scen", None, ("row", "col")),
        P("scen"),
        P("scen"),
        P(),
    )
    out_specs = (P("scen", ("row", "col")), P("scen", ("row", "col")))
    return jax.shard_map(body, mesh=mesh, in_specs=in_specs, out_specs=out_specs, check_vma=False)
```

```python
import jax
import jax.numpy as jnp
from jax import lax
from jax.experimental import pallas as pl
from jax.experimental.pallas import tpu as pltpu
from jax.sharding import PartitionSpec as P

AXES = ("scen", "row", "col")
HIGH = lax.Precision.HIGH
HIGHEST = lax.Precision.HIGHEST
HORNER = 7


def place(device):
    scen, rest = divmod(device, 16)
    r, c = divmod(rest, 8)
    return (scen // 4, scen % 4, r, c // 2, c % 2)


def number(zl, x, r, y, h):
    return ((zl % 4) * 4 + x % 4) * 16 + (r % 2) * 8 + (y % 4) * 2 + h % 2


def block_of(r, y, h):
    return (r % 2) * 8 + (y % 4) * 2 + h % 2


def send(value, where):
    pairs = []
    for device in range(256):
        target = where(*place(device))
        if target is not None:
            pairs.append((device, target))
    return lax.ppermute(value, AXES, pairs)


def to_core(zl, x, r, y, h):
    return number(zl, x, r + 1, y, h)


def to_far(zl, x, r, y, h):
    return number(zl, x, r, y, h + 1)


def to_y(step):
    return lambda zl, x, r, y, h: number(zl, x, r, y + step, h)


def to_x(step):
    return lambda zl, x, r, y, h: number(zl, x + step, r, y, h)


def to_z(step):
    return lambda zl, x, r, y, h: number(zl + step, x, r, y, h)


def to_pair(zl, x, r, y, h):
    return number(zl, x ^ 1, r, y, h)


def pick(array, index, axis=0):
    return lax.dynamic_index_in_dim(array, index, axis, keepdims=False)


def flip_x(bit):
    return lambda zl, x, r, y, h: number(zl, x ^ bit, r, y, h)


def flip_z(bit):
    return lambda zl, x, r, y, h: number(zl ^ bit, x, r, y, h)


def to_stage_owner(step):
    def where(zl, x, r, y, h):
        return None if (x + step) % 4 == 3 else number(zl, x + step, r, y, h)

    return where


def final_target(mirrored):
    def where(zl, x, r, y, h):
        if x == 3 or (mirrored and x == 0):
            return None
        f, e = divmod(zl, 2)
        row, col = block_of(r ^ e, y, h), block_of(r, y + x, h ^ f)
        return col * 16 + row if mirrored else row * 16 + col

    return where


def reduce_pieces(parts, axis_index, step_of):
    total = pick(parts, axis_index)
    for step in (1, 2, 3):
        total = total + send(pick(parts, (axis_index + step) % 4), step_of(step))
    return total


def halve(value, bit, where):
    pair = value.reshape(value.shape[0], 2, value.shape[1] // 2, value.shape[2])
    return pick(pair, bit, 1) + send(pick(pair, 1 - bit, 1), where)


def double(value, bit, where):
    got = send(value, where)
    return jnp.where(
        bit == 0, jnp.concatenate([value, got], 2), jnp.concatenate([got, value], 2)
    )


def gather_kkt(rows, early, late):
    both = jnp.stack([rows, send(rows, to_far)])
    both, early = lax.optimization_barrier((both, early))
    mine = jnp.stack([both] + [send(both, to_y(-step)) for step in (1, 2, 3)])
    mine, late = lax.optimization_barrier((mine, late))
    return mine, send(mine, to_core), early, late


def split(value):
    high = value.astype(jnp.bfloat16)
    return high, (value - high.astype(jnp.float32)).astype(jnp.bfloat16)


def dot(left, right):
    return jnp.dot(left, right, preferred_element_type=jnp.float32)


def solve_kernel(
    place_ref, mine_ref, other_ref, border_ref, out_ref, high_ref, low_ref, inv_ref, now_ref
):
    r, y, h = place_ref[0], place_ref[1], place_ref[2]
    count, order = mine_ref.shape[3:]
    for core, ref in ((r, mine_ref), (1 - r, other_ref)):
        for f in range(2):
            for step in range(4):
                number = 8 * core + 2 * ((y + step) % 4) + (h + f) % 2
                start = pl.multiple_of(number * count, count)
                piece = ref[step, f, 0]
                high, low = split(piece)
                high_ref[pl.ds(start, count), :] = high
                low_ref[pl.ds(start, count), :] = low
                on_diag = lax.broadcasted_iota(
                    jnp.int32, piece.shape, 1
                ) == start + lax.broadcasted_iota(jnp.int32, piece.shape, 0)
                diag = jnp.sum(jnp.where(on_diag, piece, 0.0), axis=1, keepdims=True)
                inv_ref[pl.ds(start, count), :] = jnp.broadcast_to(1.0 / diag, (count, inv_ref.shape[1]))
    inv_diag = inv_ref[:, :1]
    now_ref[...] = inv_diag * border_ref[0]

    def step(index, carry):
        high, low = split(now_ref[...])
        product = dot(high_ref[...], high) + (dot(high_ref[...], low) + dot(low_ref[...], high))
        now_ref[...] += inv_ref[:, :1] * (border_ref[0] - product)
        return carry

    lax.fori_loop(0, HORNER, step, 0)
    out_ref[0] = now_ref[...].T


def solve(where, mine, other, border):
    slots, order, width = border.shape
    count = mine.shape[3]
    rows_spec = pl.BlockSpec(
        (4, 2, 1, count, order), lambda slot, place: (0, 0, slot, 0, 0)
    )
    border_spec = pl.BlockSpec((1, order, width), lambda slot, place: (slot, 0, 0))
    return pl.pallas_call(
        solve_kernel,
        grid_spec=pltpu.PrefetchScalarGridSpec(
            num_scalar_prefetch=1,
            grid=(slots,),
            in_specs=[rows_spec, rows_spec, border_spec],
            out_specs=pl.BlockSpec((1, width, order), lambda slot, place: (slot, 0, 0)),
            scratch_shapes=[
                pltpu.VMEM((order, order), jnp.bfloat16),
                pltpu.VMEM((order, order), jnp.bfloat16),
                pltpu.VMEM((order, 128), jnp.float32),
                pltpu.VMEM((order, width), jnp.float32),
            ],
        ),
        out_shape=jax.ShapeDtypeStruct((slots, width, order), jnp.float32),
        compiler_params=pltpu.CompilerParams(vmem_limit_bytes=40 * 2**20),
        cost_estimate=pl.CostEstimate(
            flops=2 * slots * order * order * width * 3 * HORNER,
            bytes_accessed=4 * slots * order * (order + 2 * width),
            transcendentals=0,
        ),
        name="solve",
    )(where, mine, other, border)


def exact(left, right, contracting):
    return lax.dot_general(
        left, right, (contracting, ((), ())), precision=HIGHEST, preferred_element_type=jnp.float32
    )


def factor_block(block, joint_ref):
    size = block.shape[0]
    joint_ref[...] = jnp.zeros_like(joint_ref)
    row_ids = lax.broadcasted_iota(jnp.int32, (8, size), 0)
    col_ids = lax.broadcasted_iota(jnp.int32, (8, size), 1)
    for start in range(0, size, 8):
        left = block[start : start + 8]
        right = (col_ids == row_ids + start).astype(jnp.float32)
        if start:
            done = exact(joint_ref[:, start : start + 8], joint_ref[...], ((0,), (0,)))
            left, right = left - done[:, :size], right - done[:, size:]
        columns = [
            jnp.broadcast_to(left[:, start + k : start + k + 1], (8, size)) for k in range(8)
        ]
        scale = jnp.zeros((8, size), jnp.float32)
        for k in range(8):
            pivot = jnp.broadcast_to(columns[k][k : k + 1], (8, size))
            ratio = jnp.where(row_ids > k, columns[k] / pivot, 0.0)
            for m in range(k + 1, 8):
                columns[m] = columns[m] - ratio * columns[m][k : k + 1]
            left = left - ratio * left[k : k + 1]
            right = right - ratio * right[k : k + 1]
            scale = jnp.where(row_ids == k, lax.rsqrt(pivot), scale)
        joint_ref[start : start + 8, :size] = left * scale
        joint_ref[start : start + 8, size:] = right * scale
    return joint_ref[:, size:]


def factor_kernel(place_ref, corner_ref, out_ref, work_ref, inverse_ref, joint_ref):
    h = place_ref[2]
    size = joint_ref.shape[0]
    order = work_ref.shape[0]
    width = order // 2
    cross = corner_ref[0, 1] + corner_ref[1, 1].T
    turned = cross.T
    mine = 0.5 * (corner_ref[0, 0] + corner_ref[0, 0].T)
    theirs = 0.5 * (corner_ref[1, 0] + corner_ref[1, 0].T)
    work_ref[:width, :width] = jnp.where(h == 0, mine, theirs)
    work_ref[width:, width:] = jnp.where(h == 0, theirs, mine)
    work_ref[:width, width:] = jnp.where(h == 0, cross, turned)
    work_ref[width:, :width] = jnp.where(h == 0, turned, cross)
    inverse_ref[...] = (
        lax.broadcasted_iota(jnp.int32, (order, order), 0)
        == lax.broadcasted_iota(jnp.int32, (order, order), 1)
    ).astype(jnp.float32)
    for start in range(0, order, size):
        stop = start + size
        inverse = factor_block(work_ref[start:stop, start:stop], joint_ref)
        rows = exact(inverse, inverse_ref[start:stop, :stop], ((1,), (0,)))
        inverse_ref[start:stop, :stop] = rows
        if stop < order:
            lower = exact(work_ref[stop:, start:stop], inverse, ((1,), (1,)))
            work_ref[stop:, stop:] -= exact(lower, lower, ((1,), (1,)))
            inverse_ref[stop:, :stop] -= exact(lower, rows, ((1,), (0,)))
    out_ref[...] = jnp.where(h == 0, inverse_ref[:, :width], inverse_ref[:, width:])


SCALARS = pl.BlockSpec(memory_space=pltpu.SMEM)
WHOLE = pl.BlockSpec(memory_space=pltpu.VMEM)


def factor_inverse(where, corner):
    width = corner.shape[-1]
    order = 2 * width
    size = min(128, order)
    return pl.pallas_call(
        factor_kernel,
        in_specs=[SCALARS, WHOLE],
        out_specs=WHOLE,
        out_shape=jax.ShapeDtypeStruct((order, width), jnp.float32),
        scratch_shapes=[
            pltpu.VMEM((order, order), jnp.float32),
            pltpu.VMEM((order, order), jnp.float32),
            pltpu.VMEM((size, 2 * size), jnp.float32),
        ],
        compiler_params=pltpu.CompilerParams(vmem_limit_bytes=24 * 2**20),
        cost_estimate=pl.CostEstimate(
            flops=40_000_000_000, bytes_accessed=8 * order * order, transcendentals=order
        ),
        name="factor",
    )(where, corner)


def times(left, right):
    high, low = split(right)
    return dot(left[0], high) + (dot(left[0], low) + dot(left[1], high))


def corner_kernel(place_ref, border_ref, first_ref, mid_ref, turned_ref, diag_ref, out_ref):
    h = place_ref[2]
    width = out_ref.shape[-1]
    own = times(split(turned_ref[0]), border_ref[0])
    middle = split(turned_ref[1])
    own = own + times(middle, border_ref[1])
    own = own + times(split(turned_ref[2]), border_ref[2])
    eye = lax.broadcasted_iota(jnp.int32, (width, width), 0) == lax.broadcasted_iota(
        jnp.int32, (width, width), 1
    )
    out_ref[0] = own + jnp.where(eye, diag_ref[...], 0.0)
    off = times(split(turned_ref[2 * h]), first_ref[...])
    out_ref[1] = off + jnp.where(h == 0, times(middle, mid_ref[...]), 0.0)


def corner_tiles(where, border, first, mid, turned, diag):
    slots, order, width = border.shape
    return pl.pallas_call(
        corner_kernel,
        in_specs=[SCALARS] + [WHOLE] * 5,
        out_specs=WHOLE,
        out_shape=jax.ShapeDtypeStruct((2, width, width), jnp.float32),
        compiler_params=pltpu.CompilerParams(vmem_limit_bytes=32 * 2**20),
        cost_estimate=pl.CostEstimate(
            flops=2 * 15 * order * width * width, bytes_accessed=32 * order * width, transcendentals=0
        ),
        name="corner",
    )(where, border, first, mid, turned, diag)


def stage_kernel(place_ref, *refs):
    wide_stage = len(refs) == 9
    if wide_stage:
        own_ref, first_ref, mid_ref, last_ref, turned_ref, other_ref, diag_ref, out_ref, left_ref = refs
    else:
        own_ref, first_ref, mid_ref, turned_ref, other_ref, out_ref, left_ref = refs
    y, h = place_ref[1], place_ref[2]
    slots, width, order = turned_ref.shape
    for slot in range(slots):
        for part, ref in enumerate((turned_ref, other_ref)):
            high, low = split(ref[slot])
            left_ref[0, slot, part * width : (part + 1) * width] = high
            left_ref[1, slot, part * width : (part + 1) * width] = low

    def term(slot, right):
        return times((left_ref[0, slot], left_ref[1, slot]), right)

    far = term(2 * h, first_ref[...])
    middle = term(1, mid_ref[...])
    if wide_stage:
        near = term(0, own_ref[0]) + term(1, own_ref[1]) + term(2, own_ref[2])
        far = far + middle + term(2 - 2 * h, last_ref[...])
        eye = lax.broadcasted_iota(jnp.int32, (width, width), 0) == lax.broadcasted_iota(
            jnp.int32, (width, width), 1
        )
        out_ref[0] = near[:width] + jnp.where(eye, diag_ref[...], 0.0)
    else:
        near = term(2 * (y // 2), own_ref[...]) + jnp.where(y < 2, middle, 0.0)
        far = far + jnp.where(y < 2, 0.0, middle)
        out_ref[0] = near[:width]
    out_ref[1] = near[width:]
    out_ref[2] = far[:width]
    out_ref[3] = far[width:]


def stage_tiles(where, rights, turned, other, diag=None):
    slots, width, order = turned.shape
    operands = [*rights, turned, other] + ([diag] if diag is not None else [])
    terms = 6 if diag is not None else 3
    return pl.pallas_call(
        stage_kernel,
        in_specs=[SCALARS] + [WHOLE] * len(operands),
        out_specs=WHOLE,
        out_shape=jax.ShapeDtypeStruct((4, width, width), jnp.float32),
        scratch_shapes=[pltpu.VMEM((2, slots, 2 * width, order), jnp.bfloat16)],
        compiler_params=pltpu.CompilerParams(vmem_limit_bytes=48 * 2**20),
        cost_estimate=pl.CostEstimate(
            flops=2 * 3 * terms * order * width * 2 * width,
            bytes_accessed=4 * (terms + 6) * order * width,
            transcendentals=0,
        ),
        name="stage",
    )(where, *operands)


def body(kkt, border, first_diag, assignment, panel):
    scen_index = lax.axis_index("scen")
    own_index = lax.axis_index(("row", "col"))
    zl, x = scen_index // 4, scen_index % 4
    r, y, h = own_index // 8, (own_index // 2) % 4, own_index % 2
    where = jnp.stack([r, y, h]).astype(jnp.int32)
    slots, order, width = border.shape
    first, last = 2 * h, 2 - 2 * h
    lead = 2 * (y // 2)
    diag = jnp.where(scen_index == own_index, first_diag, 0.0)[None, :]

    own_one = send(border, to_y(-1))
    far_first = send(pick(border, last), to_far)
    own_hop = send(pick(border, 2 - lead), to_y(1))

    swapped = send(kkt, to_pair)
    ids = scen_index * slots + jnp.arange(slots, dtype=jnp.int32)
    rows = jnp.where((assignment == ids)[:, None, None], kkt, swapped)
    mine, theirs, own_hop, (own_one, far_first) = gather_kkt(rows, own_hop, (own_one, far_first))
    own_two = send(own_hop, to_y(1))

    far_mid = send(border[1], to_far)
    far_last = send(pick(border, first), to_far)
    far_two = send(send(far_first, to_y(1)), to_y(1))
    far_pair_one = send(jnp.stack([far_first, far_mid]), to_y(-1))
    shared_two = send(jnp.where(y < 2, far_mid, border[1]), to_y(2))
    far_last_one = send(far_last, to_y(-1))

    mine, own_two = lax.optimization_barrier((mine, own_two))
    turned = solve(where, mine, theirs, border)
    other = send(turned, to_core)

    corner = corner_tiles(where, border, far_first, far_mid, turned, diag)
    corner = halve(corner, x % 2, flip_x(1))
    corner = halve(corner, x // 2, flip_x(2))
    corner = halve(corner, zl % 2, flip_z(1))
    corner = halve(corner, zl // 2, flip_z(2))
    corner, far_last, far_two, other = lax.optimization_barrier((corner, far_last, far_two, other))
    corner = jnp.stack([corner, send(corner, to_far)])
    corner = double(corner, zl // 2, flip_z(2))
    corner = double(corner, zl % 2, flip_z(1))
    corner = double(corner, x // 2, flip_x(2))
    corner = double(corner, x % 2, flip_x(1))

    stages = jnp.stack(
        [
            stage_tiles(where, (border, far_first, far_mid, far_last), turned, other, diag),
            stage_tiles(
                where,
                (own_one, far_pair_one[0], far_pair_one[1], far_last_one),
                turned,
                other,
                jnp.zeros_like(diag),
            ),
            stage_tiles(where, (own_two, far_two, shared_two), turned, other),
        ]
    )
    corner, stages = lax.optimization_barrier((corner, stages))
    inverse_cols = factor_inverse(where, corner)

    total = pick(stages, jnp.minimum(x, 2))
    got = [
        send(pick(stages, jnp.minimum((x + step) % 4, 2)), to_stage_owner(step))
        for step in (1, 2, 3)
    ]
    got, inverse_cols = lax.optimization_barrier((got, inverse_cols))
    total = reduce_pieces(total + got[0] + got[1] + got[2], zl, to_z)
    direct = send(total, final_target(False))
    mirrored = send(total, final_target(True))
    schur = direct + mirrored.T

    share = 2 * width // 16
    term = lax.dot_general(
        inverse_cols, schur, (((1,), (1,)), ((), ())), precision=HIGHEST,
        preferred_element_type=jnp.float32,
    )
    term = jnp.where(own_index // 2 == panel[0], term, 0.0).reshape(16, share, width)
    shares = lax.all_to_all(term, ("row", "col"), 0, 0, tiled=True)
    chosen = lax.dynamic_slice_in_dim(shares, 2 * panel[0], 2, 0)
    return (schur, (chosen[0] + chosen[1]).T)


def solution(mesh):
    in_specs = (
        P("scen", ("row", "col"), None),
        P("scen", None, ("row", "col")),
        P("scen"),
        P("scen"),
        P(),
    )
    out_specs = (P("scen", ("row", "col")), P("scen", ("row", "col")))
    return jax.shard_map(body, mesh=mesh, in_specs=in_specs, out_specs=out_specs, check_vma=False)
```

```python
import jax
import jax.numpy as jnp
from jax import lax
from jax.experimental import pallas as pl
from jax.experimental.pallas import tpu as pltpu
from jax.sharding import PartitionSpec as P

AXES = ("scen", "row", "col")
HIGH = lax.Precision.HIGH
HIGHEST = lax.Precision.HIGHEST
HORNER = 7


def place(device):
    scen, rest = divmod(device, 16)
    r, c = divmod(rest, 8)
    return (scen // 4, scen % 4, r, c // 2, c % 2)


def number(zl, x, r, y, h):
    return ((zl % 4) * 4 + x % 4) * 16 + (r % 2) * 8 + (y % 4) * 2 + h % 2


def block_of(r, y, h):
    return (r % 2) * 8 + (y % 4) * 2 + h % 2


def send(value, where):
    pairs = []
    for device in range(256):
        target = where(*place(device))
        if target is not None:
            pairs.append((device, target))
    return lax.ppermute(value, AXES, pairs)


def to_core(zl, x, r, y, h):
    return number(zl, x, r + 1, y, h)


def to_far(zl, x, r, y, h):
    return number(zl, x, r, y, h + 1)


def to_y(step):
    return lambda zl, x, r, y, h: number(zl, x, r, y + step, h)


def to_x(step):
    return lambda zl, x, r, y, h: number(zl, x + step, r, y, h)


def to_z(step):
    return lambda zl, x, r, y, h: number(zl + step, x, r, y, h)


def to_pair(zl, x, r, y, h):
    return number(zl, x ^ 1, r, y, h)


def pick(array, index, axis=0):
    return lax.dynamic_index_in_dim(array, index, axis, keepdims=False)


def flip_x(bit):
    return lambda zl, x, r, y, h: number(zl, x ^ bit, r, y, h)


def flip_z(bit):
    return lambda zl, x, r, y, h: number(zl ^ bit, x, r, y, h)


def to_stage_owner(step):
    def where(zl, x, r, y, h):
        return None if (x + step) % 4 == 3 else number(zl, x + step, r, y, h)

    return where


def final_target(mirrored):
    def where(zl, x, r, y, h):
        if x == 3 or (mirrored and x == 0):
            return None
        f, e = divmod(zl, 2)
        row, col = block_of(r ^ e, y, h), block_of(r, y + x, h ^ f)
        return col * 16 + row if mirrored else row * 16 + col

    return where


def reduce_pieces(parts, axis_index, step_of):
    total = pick(parts, axis_index)
    for step in (1, 2, 3):
        total = total + send(pick(parts, (axis_index + step) % 4), step_of(step))
    return total


def halve(value, bit, where):
    pair = value.reshape(value.shape[0], 2, value.shape[1] // 2, value.shape[2])
    return pick(pair, bit, 1) + send(pick(pair, 1 - bit, 1), where)


def double(value, bit, where):
    got = send(value, where)
    return jnp.where(
        bit == 0, jnp.concatenate([value, got], 2), jnp.concatenate([got, value], 2)
    )


def split(value):
    high = value.astype(jnp.bfloat16)
    return high, (value - high.astype(jnp.float32)).astype(jnp.bfloat16)


def dot(left, right):
    return jnp.dot(left, right, preferred_element_type=jnp.float32)


def solve_kernel(
    place_ref, mine_ref, other_ref, border_ref, out_ref, high_ref, low_ref, inv_ref, now_ref
):
    r, y, h = place_ref[0], place_ref[1], place_ref[2]
    count, order = mine_ref.shape[3:]
    for core, ref in ((r, mine_ref), (1 - r, other_ref)):
        for f in range(2):
            for step in range(4):
                number = 8 * core + 2 * ((y + step) % 4) + (h + f) % 2
                start = pl.multiple_of(number * count, count)
                piece = ref[step, f, 0]
                high, low = split(piece)
                high_ref[pl.ds(start, count), :] = high
                low_ref[pl.ds(start, count), :] = low
                on_diag = lax.broadcasted_iota(
                    jnp.int32, piece.shape, 1
                ) == start + lax.broadcasted_iota(jnp.int32, piece.shape, 0)
                diag = jnp.sum(jnp.where(on_diag, piece, 0.0), axis=1, keepdims=True)
                inv_ref[pl.ds(start, count), :] = jnp.broadcast_to(1.0 / diag, (count, inv_ref.shape[1]))
    inv_diag = inv_ref[:, :1]
    now_ref[...] = inv_diag * border_ref[0]

    def step(index, carry):
        high, low = split(now_ref[...])
        product = dot(high_ref[...], high) + (dot(high_ref[...], low) + dot(low_ref[...], high))
        now_ref[...] += inv_ref[:, :1] * (border_ref[0] - product)
        return carry

    lax.fori_loop(0, HORNER, step, 0)
    out_ref[0] = now_ref[...].T


def solve(where, mine, other, border):
    slots, order, width = border.shape
    count = mine.shape[3]
    rows_spec = pl.BlockSpec(
        (4, 2, 1, count, order), lambda slot, place: (0, 0, slot, 0, 0)
    )
    border_spec = pl.BlockSpec((1, order, width), lambda slot, place: (slot, 0, 0))
    return pl.pallas_call(
        solve_kernel,
        grid_spec=pltpu.PrefetchScalarGridSpec(
            num_scalar_prefetch=1,
            grid=(slots,),
            in_specs=[rows_spec, rows_spec, border_spec],
            out_specs=pl.BlockSpec((1, width, order), lambda slot, place: (slot, 0, 0)),
            scratch_shapes=[
                pltpu.VMEM((order, order), jnp.bfloat16),
                pltpu.VMEM((order, order), jnp.bfloat16),
                pltpu.VMEM((order, 128), jnp.float32),
                pltpu.VMEM((order, width), jnp.float32),
            ],
        ),
        out_shape=jax.ShapeDtypeStruct((slots, width, order), jnp.float32),
        compiler_params=pltpu.CompilerParams(vmem_limit_bytes=40 * 2**20),
        cost_estimate=pl.CostEstimate(
            flops=2 * slots * order * order * width * 3 * HORNER,
            bytes_accessed=4 * slots * order * (order + 2 * width),
            transcendentals=0,
        ),
        name="solve",
    )(where, mine, other, border)


def exact(left, right, contracting):
    return lax.dot_general(
        left, right, (contracting, ((), ())), precision=HIGHEST, preferred_element_type=jnp.float32
    )


def factor_block(block, joint_ref):
    size = block.shape[0]
    joint_ref[...] = jnp.zeros_like(joint_ref)
    row_ids = lax.broadcasted_iota(jnp.int32, (8, size), 0)
    col_ids = lax.broadcasted_iota(jnp.int32, (8, size), 1)
    for start in range(0, size, 8):
        left = block[start : start + 8]
        right = (col_ids == row_ids + start).astype(jnp.float32)
        if start:
            done = exact(joint_ref[:, start : start + 8], joint_ref[...], ((0,), (0,)))
            left, right = left - done[:, :size], right - done[:, size:]
        columns = [
            jnp.broadcast_to(left[:, start + k : start + k + 1], (8, size)) for k in range(8)
        ]
        scale = jnp.zeros((8, size), jnp.float32)
        for k in range(8):
            pivot = jnp.broadcast_to(columns[k][k : k + 1], (8, size))
            ratio = jnp.where(row_ids > k, columns[k] / pivot, 0.0)
            for m in range(k + 1, 8):
                columns[m] = columns[m] - ratio * columns[m][k : k + 1]
            left = left - ratio * left[k : k + 1]
            right = right - ratio * right[k : k + 1]
            scale = jnp.where(row_ids == k, lax.rsqrt(pivot), scale)
        joint_ref[start : start + 8, :size] = left * scale
        joint_ref[start : start + 8, size:] = right * scale
    return joint_ref[:, size:]


def factor_kernel(place_ref, corner_ref, out_ref, work_ref, inverse_ref, joint_ref):
    h = place_ref[2]
    size = joint_ref.shape[0]
    order = work_ref.shape[0]
    width = order // 2
    cross = corner_ref[0, 1] + corner_ref[1, 1].T
    turned = cross.T
    mine = 0.5 * (corner_ref[0, 0] + corner_ref[0, 0].T)
    theirs = 0.5 * (corner_ref[1, 0] + corner_ref[1, 0].T)
    work_ref[:width, :width] = jnp.where(h == 0, mine, theirs)
    work_ref[width:, width:] = jnp.where(h == 0, theirs, mine)
    work_ref[:width, width:] = jnp.where(h == 0, cross, turned)
    work_ref[width:, :width] = jnp.where(h == 0, turned, cross)
    inverse_ref[...] = (
        lax.broadcasted_iota(jnp.int32, (order, order), 0)
        == lax.broadcasted_iota(jnp.int32, (order, order), 1)
    ).astype(jnp.float32)
    for start in range(0, order, size):
        stop = start + size
        inverse = factor_block(work_ref[start:stop, start:stop], joint_ref)
        rows = exact(inverse, inverse_ref[start:stop, :stop], ((1,), (0,)))
        inverse_ref[start:stop, :stop] = rows
        if stop < order:
            lower = exact(work_ref[stop:, start:stop], inverse, ((1,), (1,)))
            work_ref[stop:, stop:] -= exact(lower, lower, ((1,), (1,)))
            inverse_ref[stop:, :stop] -= exact(lower, rows, ((1,), (0,)))
    out_ref[...] = jnp.where(h == 0, inverse_ref[:, :width], inverse_ref[:, width:])


SCALARS = pl.BlockSpec(memory_space=pltpu.SMEM)
WHOLE = pl.BlockSpec(memory_space=pltpu.VMEM)


def factor_inverse(where, corner):
    width = corner.shape[-1]
    order = 2 * width
    size = min(128, order)
    return pl.pallas_call(
        factor_kernel,
        in_specs=[SCALARS, WHOLE],
        out_specs=WHOLE,
        out_shape=jax.ShapeDtypeStruct((order, width), jnp.float32),
        scratch_shapes=[
            pltpu.VMEM((order, order), jnp.float32),
            pltpu.VMEM((order, order), jnp.float32),
            pltpu.VMEM((size, 2 * size), jnp.float32),
        ],
        compiler_params=pltpu.CompilerParams(vmem_limit_bytes=24 * 2**20),
        cost_estimate=pl.CostEstimate(
            flops=40_000_000_000, bytes_accessed=8 * order * order, transcendentals=order
        ),
        name="factor",
    )(where, corner)


def times(left, right):
    high, low = split(right)
    return dot(left[0], high) + (dot(left[0], low) + dot(left[1], high))


def corner_kernel(place_ref, border_ref, first_ref, mid_ref, turned_ref, diag_ref, out_ref):
    h = place_ref[2]
    width = out_ref.shape[-1]
    own = times(split(turned_ref[0]), border_ref[0])
    middle = split(turned_ref[1])
    own = own + times(middle, border_ref[1])
    own = own + times(split(turned_ref[2]), border_ref[2])
    eye = lax.broadcasted_iota(jnp.int32, (width, width), 0) == lax.broadcasted_iota(
        jnp.int32, (width, width), 1
    )
    out_ref[0] = own + jnp.where(eye, diag_ref[...], 0.0)
    off = times(split(turned_ref[2 * h]), first_ref[...])
    out_ref[1] = off + jnp.where(h == 0, times(middle, mid_ref[...]), 0.0)


def corner_tiles(where, border, first, mid, turned, diag):
    slots, order, width = border.shape
    return pl.pallas_call(
        corner_kernel,
        in_specs=[SCALARS] + [WHOLE] * 5,
        out_specs=WHOLE,
        out_shape=jax.ShapeDtypeStruct((2, width, width), jnp.float32),
        compiler_params=pltpu.CompilerParams(vmem_limit_bytes=32 * 2**20),
        cost_estimate=pl.CostEstimate(
            flops=2 * 15 * order * width * width, bytes_accessed=32 * order * width, transcendentals=0
        ),
        name="corner",
    )(where, border, first, mid, turned, diag)


def stage_kernel(place_ref, *refs):
    wide_stage = len(refs) == 10
    if wide_stage:
        head_ref, tail_ref, first_ref, mid_ref, last_ref, turned_ref, other_ref, diag_ref, out_ref, left_ref = refs
    else:
        own_ref, first_ref, mid_ref, turned_ref, other_ref, out_ref, left_ref = refs
    y, h = place_ref[1], place_ref[2]
    slots, width, order = turned_ref.shape
    for slot in range(slots):
        for part, ref in enumerate((turned_ref, other_ref)):
            high, low = split(ref[slot])
            left_ref[0, slot, part * width : (part + 1) * width] = high
            left_ref[1, slot, part * width : (part + 1) * width] = low

    def term(slot, right):
        return times((left_ref[0, slot], left_ref[1, slot]), right)

    far = term(2 * h, first_ref[...])
    middle = term(1, mid_ref[...])
    if wide_stage:
        near = term(0, head_ref[...]) + term(1, tail_ref[0]) + term(2, tail_ref[1])
        far = far + middle + term(2 - 2 * h, last_ref[...])
        eye = lax.broadcasted_iota(jnp.int32, (width, width), 0) == lax.broadcasted_iota(
            jnp.int32, (width, width), 1
        )
        out_ref[0] = near[:width] + jnp.where(eye, diag_ref[...], 0.0)
    else:
        near = term(2 * (y // 2), own_ref[...]) + jnp.where(y < 2, middle, 0.0)
        far = far + jnp.where(y < 2, 0.0, middle)
        out_ref[0] = near[:width]
    out_ref[1] = near[width:]
    out_ref[2] = far[:width]
    out_ref[3] = far[width:]


def stage_tiles(where, rights, turned, other, diag=None):
    slots, width, order = turned.shape
    operands = [*rights, turned, other] + ([diag] if diag is not None else [])
    terms = 6 if diag is not None else 3
    return pl.pallas_call(
        stage_kernel,
        in_specs=[SCALARS] + [WHOLE] * len(operands),
        out_specs=WHOLE,
        out_shape=jax.ShapeDtypeStruct((4, width, width), jnp.float32),
        scratch_shapes=[pltpu.VMEM((2, slots, 2 * width, order), jnp.bfloat16)],
        compiler_params=pltpu.CompilerParams(vmem_limit_bytes=48 * 2**20),
        cost_estimate=pl.CostEstimate(
            flops=2 * 3 * terms * order * width * 2 * width,
            bytes_accessed=4 * (terms + 6) * order * width,
            transcendentals=0,
        ),
        name="stage",
    )(where, *operands)


def body(kkt, border, first_diag, assignment, panel):
    scen_index = lax.axis_index("scen")
    own_index = lax.axis_index(("row", "col"))
    zl, x = scen_index // 4, scen_index % 4
    r, y, h = own_index // 8, (own_index // 2) % 4, own_index % 2
    where = jnp.stack([r, y, h]).astype(jnp.int32)
    slots, order, width = border.shape
    first, last = 2 * h, 2 - 2 * h
    lead = 2 * (y // 2)
    diag = jnp.where(scen_index == own_index, first_diag, 0.0)[None, :]

    barrier = lax.optimization_barrier
    own_one_head = send(border[0], to_y(-1))
    own_hop = send(pick(border, 2 - lead), to_y(1))

    swapped = send(kkt, to_pair)
    ids = scen_index * slots + jnp.arange(slots, dtype=jnp.int32)
    rows = jnp.where((assignment == ids)[:, None, None], kkt, swapped)
    both = jnp.stack([rows, send(rows, to_far)])
    both, own_hop, own_one_head = barrier((both, own_hop, own_one_head))
    mine = jnp.stack([both] + [send(both, to_y(-step)) for step in (1, 2, 3)])
    far_first = send(pick(border, last), to_far)
    mine, far_first, tail = barrier((mine, far_first, border[1:]))
    theirs = send(mine, to_core)

    own_one_tail = send(tail, to_y(-1))
    own_two = send(own_hop, to_y(1))
    far_hop = send(far_first, to_y(1))
    far_mid = send(tail[0], to_far)
    turned = solve(where, mine, theirs, border)
    turned, far_mid, far_hop, own_two, own_one_tail = barrier(
        (turned, far_mid, far_hop, own_two, own_one_tail)
    )
    other = send(turned, to_core)
    far_last = send(pick(border, first), to_far)
    far_two = send(far_hop, to_y(1))
    far_pair_one = send(jnp.stack([far_first, far_mid]), to_y(-1))
    shared_two = send(jnp.where(y < 2, far_mid, tail[0]), to_y(2))

    corner = corner_tiles(where, border, far_first, far_mid, turned, diag)
    corner = halve(corner, x % 2, flip_x(1))
    corner = halve(corner, x // 2, flip_x(2))
    corner, far_last, far_two, other = barrier((corner, far_last, far_two, other))
    far_last_one = send(far_last, to_y(-1))
    corner = halve(corner, zl % 2, flip_z(1))
    corner = halve(corner, zl // 2, flip_z(2))
    corner = jnp.stack([corner, send(corner, to_far)])
    corner = double(corner, zl // 2, flip_z(2))
    corner = double(corner, zl % 2, flip_z(1))
    corner = double(corner, x // 2, flip_x(2))
    corner = double(corner, x % 2, flip_x(1))

    stages = jnp.stack(
        [
            stage_tiles(where, (border[0], tail, far_first, far_mid, far_last), turned, other, diag),
            stage_tiles(
                where,
                (own_one_head, own_one_tail, far_pair_one[0], far_pair_one[1], far_last_one),
                turned,
                other,
                jnp.zeros_like(diag),
            ),
            stage_tiles(where, (own_two, far_two, shared_two), turned, other),
        ]
    )
    corner, stages = lax.optimization_barrier((corner, stages))
    inverse_cols = factor_inverse(where, corner)

    total = pick(stages, jnp.minimum(x, 2))
    got = [
        send(pick(stages, jnp.minimum((x + step) % 4, 2)), to_stage_owner(step))
        for step in (1, 2, 3)
    ]
    got, inverse_cols = lax.optimization_barrier((got, inverse_cols))
    total = reduce_pieces(total + got[0] + got[1] + got[2], zl, to_z)
    direct = send(total, final_target(False))
    mirrored = send(total, final_target(True))
    schur = direct + mirrored.T

    share = 2 * width // 16
    term = lax.dot_general(
        inverse_cols, schur, (((1,), (1,)), ((), ())), precision=HIGHEST,
        preferred_element_type=jnp.float32,
    )
    term = jnp.where(own_index // 2 == panel[0], term, 0.0).reshape(16, share, width)
    shares = lax.all_to_all(term, ("row", "col"), 0, 0, tiled=True)
    chosen = lax.dynamic_slice_in_dim(shares, 2 * panel[0], 2, 0)
    return (schur, (chosen[0] + chosen[1]).T)


def solution(mesh):
    in_specs = (
        P("scen", ("row", "col"), None),
        P("scen", None, ("row", "col")),
        P("scen"),
        P("scen"),
        P(),
    )
    out_specs = (P("scen", ("row", "col")), P("scen", ("row", "col")))
    return jax.shard_map(body, mesh=mesh, in_specs=in_specs, out_specs=out_specs, check_vma=False)
```

```python
import jax
import jax.numpy as jnp
from jax import lax
from jax.experimental import pallas as pl
from jax.experimental.pallas import tpu as pltpu
from jax.sharding import PartitionSpec as P

AXES = ("scen", "row", "col")
HIGH = lax.Precision.HIGH
HIGHEST = lax.Precision.HIGHEST
HORNER = 7


def place(device):
    scen, rest = divmod(device, 16)
    r, c = divmod(rest, 8)
    return (scen // 4, scen % 4, r, c // 2, c % 2)


def number(zl, x, r, y, h):
    return ((zl % 4) * 4 + x % 4) * 16 + (r % 2) * 8 + (y % 4) * 2 + h % 2


def block_of(r, y, h):
    return (r % 2) * 8 + (y % 4) * 2 + h % 2


def send(value, where):
    pairs = []
    for device in range(256):
        target = where(*place(device))
        if target is not None:
            pairs.append((device, target))
    return lax.ppermute(value, AXES, pairs)


def to_core(zl, x, r, y, h):
    return number(zl, x, r + 1, y, h)


def to_far(zl, x, r, y, h):
    return number(zl, x, r, y, h + 1)


def to_y(step):
    return lambda zl, x, r, y, h: number(zl, x, r, y + step, h)


def to_x(step):
    return lambda zl, x, r, y, h: number(zl, x + step, r, y, h)


def to_z(step):
    return lambda zl, x, r, y, h: number(zl + step, x, r, y, h)


def to_pair(zl, x, r, y, h):
    return number(zl, x ^ 1, r, y, h)


def pick(array, index, axis=0):
    return lax.dynamic_index_in_dim(array, index, axis, keepdims=False)


def flip_x(bit):
    return lambda zl, x, r, y, h: number(zl, x ^ bit, r, y, h)


def flip_z(bit):
    return lambda zl, x, r, y, h: number(zl ^ bit, x, r, y, h)


def to_stage_owner(step):
    def where(zl, x, r, y, h):
        return None if (x + step) % 4 == 3 else number(zl, x + step, r, y, h)

    return where


def final_target(mirrored):
    def where(zl, x, r, y, h):
        if x == 3 or (mirrored and x == 0):
            return None
        f, e = divmod(zl, 2)
        row, col = block_of(r ^ e, y, h), block_of(r, y + x, h ^ f)
        return col * 16 + row if mirrored else row * 16 + col

    return where


def reduce_pieces(parts, axis_index, step_of):
    total = pick(parts, axis_index)
    for step in (1, 2, 3):
        total = total + send(pick(parts, (axis_index + step) % 4), step_of(step))
    return total


def halve(value, bit, where):
    pair = value.reshape(value.shape[0], 2, value.shape[1] // 2, value.shape[2])
    return pick(pair, bit, 1) + send(pick(pair, 1 - bit, 1), where)


def double(value, bit, where):
    got = send(value, where)
    return jnp.where(
        bit == 0, jnp.concatenate([value, got], 2), jnp.concatenate([got, value], 2)
    )


def split(value):
    high = value.astype(jnp.bfloat16)
    return high, (value - high.astype(jnp.float32)).astype(jnp.bfloat16)


def dot(left, right):
    return jnp.dot(left, right, preferred_element_type=jnp.float32)


def solve_kernel(
    place_ref, mine_ref, other_ref, border_ref, out_ref, high_ref, low_ref, inv_ref, now_ref
):
    r, y, h = place_ref[0], place_ref[1], place_ref[2]
    count, order = mine_ref.shape[3:]
    for core, ref in ((r, mine_ref), (1 - r, other_ref)):
        for f in range(2):
            for step in range(4):
                number = 8 * core + 2 * ((y + step) % 4) + (h + f) % 2
                start = pl.multiple_of(number * count, count)
                piece = ref[step, f, 0]
                high, low = split(piece)
                high_ref[pl.ds(start, count), :] = high
                low_ref[pl.ds(start, count), :] = low
                on_diag = lax.broadcasted_iota(
                    jnp.int32, piece.shape, 1
                ) == start + lax.broadcasted_iota(jnp.int32, piece.shape, 0)
                diag = jnp.sum(jnp.where(on_diag, piece, 0.0), axis=1, keepdims=True)
                inv_ref[pl.ds(start, count), :] = jnp.broadcast_to(1.0 / diag, (count, inv_ref.shape[1]))
    inv_diag = inv_ref[:, :1]
    now_ref[...] = inv_diag * border_ref[0]

    def step(index, carry):
        high, low = split(now_ref[...])
        product = dot(high_ref[...], high) + (dot(high_ref[...], low) + dot(low_ref[...], high))
        now_ref[...] += inv_ref[:, :1] * (border_ref[0] - product)
        return carry

    lax.fori_loop(0, HORNER, step, 0)
    out_ref[0] = now_ref[...].T


def solve(where, mine, other, border):
    slots, order, width = border.shape
    count = mine.shape[3]
    rows_spec = pl.BlockSpec(
        (4, 2, 1, count, order), lambda slot, place: (0, 0, slot, 0, 0)
    )
    border_spec = pl.BlockSpec((1, order, width), lambda slot, place: (slot, 0, 0))
    return pl.pallas_call(
        solve_kernel,
        grid_spec=pltpu.PrefetchScalarGridSpec(
            num_scalar_prefetch=1,
            grid=(slots,),
            in_specs=[rows_spec, rows_spec, border_spec],
            out_specs=pl.BlockSpec((1, width, order), lambda slot, place: (slot, 0, 0)),
            scratch_shapes=[
                pltpu.VMEM((order, order), jnp.bfloat16),
                pltpu.VMEM((order, order), jnp.bfloat16),
                pltpu.VMEM((order, 128), jnp.float32),
                pltpu.VMEM((order, width), jnp.float32),
            ],
        ),
        out_shape=jax.ShapeDtypeStruct((slots, width, order), jnp.float32),
        compiler_params=pltpu.CompilerParams(vmem_limit_bytes=40 * 2**20),
        cost_estimate=pl.CostEstimate(
            flops=2 * slots * order * order * width,
            bytes_accessed=4 * slots * order * (order + 2 * width),
            transcendentals=0,
        ),
        name="solve",
    )(where, mine, other, border)


def exact(left, right, contracting):
    return lax.dot_general(
        left, right, (contracting, ((), ())), precision=HIGHEST, preferred_element_type=jnp.float32
    )


def factor_block(block, joint_ref):
    size = block.shape[0]
    joint_ref[...] = jnp.zeros_like(joint_ref)
    row_ids = lax.broadcasted_iota(jnp.int32, (8, size), 0)
    col_ids = lax.broadcasted_iota(jnp.int32, (8, size), 1)
    for start in range(0, size, 8):
        left = block[start : start + 8]
        right = (col_ids == row_ids + start).astype(jnp.float32)
        if start:
            done = exact(joint_ref[:, start : start + 8], joint_ref[...], ((0,), (0,)))
            left, right = left - done[:, :size], right - done[:, size:]
        columns = [
            jnp.broadcast_to(left[:, start + k : start + k + 1], (8, size)) for k in range(8)
        ]
        scale = jnp.zeros((8, size), jnp.float32)
        for k in range(8):
            pivot = jnp.broadcast_to(columns[k][k : k + 1], (8, size))
            ratio = jnp.where(row_ids > k, columns[k] / pivot, 0.0)
            for m in range(k + 1, 8):
                columns[m] = columns[m] - ratio * columns[m][k : k + 1]
            left = left - ratio * left[k : k + 1]
            right = right - ratio * right[k : k + 1]
            scale = jnp.where(row_ids == k, lax.rsqrt(pivot), scale)
        joint_ref[start : start + 8, :size] = left * scale
        joint_ref[start : start + 8, size:] = right * scale
    return joint_ref[:, size:]


def factor_kernel(place_ref, corner_ref, out_ref, work_ref, inverse_ref, joint_ref):
    h = place_ref[2]
    size = joint_ref.shape[0]
    order = work_ref.shape[0]
    width = order // 2
    cross = corner_ref[0, 1] + corner_ref[1, 1].T
    turned = cross.T
    mine = 0.5 * (corner_ref[0, 0] + corner_ref[0, 0].T)
    theirs = 0.5 * (corner_ref[1, 0] + corner_ref[1, 0].T)
    work_ref[:width, :width] = jnp.where(h == 0, mine, theirs)
    work_ref[width:, width:] = jnp.where(h == 0, theirs, mine)
    work_ref[:width, width:] = jnp.where(h == 0, cross, turned)
    work_ref[width:, :width] = jnp.where(h == 0, turned, cross)
    inverse_ref[...] = (
        lax.broadcasted_iota(jnp.int32, (order, order), 0)
        == lax.broadcasted_iota(jnp.int32, (order, order), 1)
    ).astype(jnp.float32)
    for start in range(0, order, size):
        stop = start + size
        inverse = factor_block(work_ref[start:stop, start:stop], joint_ref)
        rows = exact(inverse, inverse_ref[start:stop, :stop], ((1,), (0,)))
        inverse_ref[start:stop, :stop] = rows
        if stop < order:
            lower = exact(work_ref[stop:, start:stop], inverse, ((1,), (1,)))
            work_ref[stop:, stop:] -= exact(lower, lower, ((1,), (1,)))
            inverse_ref[stop:, :stop] -= exact(lower, rows, ((1,), (0,)))
    out_ref[...] = jnp.where(h == 0, inverse_ref[:, :width], inverse_ref[:, width:])


SCALARS = pl.BlockSpec(memory_space=pltpu.SMEM)
WHOLE = pl.BlockSpec(memory_space=pltpu.VMEM)


def factor_inverse(where, corner):
    width = corner.shape[-1]
    order = 2 * width
    size = min(128, order)
    return pl.pallas_call(
        factor_kernel,
        in_specs=[SCALARS, WHOLE],
        out_specs=WHOLE,
        out_shape=jax.ShapeDtypeStruct((order, width), jnp.float32),
        scratch_shapes=[
            pltpu.VMEM((order, order), jnp.float32),
            pltpu.VMEM((order, order), jnp.float32),
            pltpu.VMEM((size, 2 * size), jnp.float32),
        ],
        compiler_params=pltpu.CompilerParams(vmem_limit_bytes=24 * 2**20),
        cost_estimate=pl.CostEstimate(
            flops=40_000_000_000, bytes_accessed=8 * order * order, transcendentals=order
        ),
        name="factor",
    )(where, corner)


def times(left, right):
    high, low = split(right)
    return dot(left[0], high) + (dot(left[0], low) + dot(left[1], high))


def corner_kernel(place_ref, border_ref, first_ref, mid_ref, turned_ref, diag_ref, out_ref):
    h = place_ref[2]
    width = out_ref.shape[-1]
    own = times(split(turned_ref[0]), border_ref[0])
    middle = split(turned_ref[1])
    own = own + times(middle, border_ref[1])
    own = own + times(split(turned_ref[2]), border_ref[2])
    eye = lax.broadcasted_iota(jnp.int32, (width, width), 0) == lax.broadcasted_iota(
        jnp.int32, (width, width), 1
    )
    out_ref[0] = own + jnp.where(eye, diag_ref[...], 0.0)
    off = times(split(turned_ref[2 * h]), first_ref[...])
    out_ref[1] = off + jnp.where(h == 0, times(middle, mid_ref[...]), 0.0)


def corner_tiles(where, border, first, mid, turned, diag):
    slots, order, width = border.shape
    return pl.pallas_call(
        corner_kernel,
        in_specs=[SCALARS] + [WHOLE] * 5,
        out_specs=WHOLE,
        out_shape=jax.ShapeDtypeStruct((2, width, width), jnp.float32),
        compiler_params=pltpu.CompilerParams(vmem_limit_bytes=32 * 2**20),
        cost_estimate=pl.CostEstimate(
            flops=2 * 15 * order * width * width, bytes_accessed=32 * order * width, transcendentals=0
        ),
        name="corner",
    )(where, border, first, mid, turned, diag)


def stage_kernel(place_ref, *refs):
    wide_stage = len(refs) == 10
    if wide_stage:
        head_ref, tail_ref, first_ref, mid_ref, last_ref, turned_ref, other_ref, diag_ref, out_ref, left_ref = refs
    else:
        own_ref, first_ref, mid_ref, turned_ref, other_ref, out_ref, left_ref = refs
    y, h = place_ref[1], place_ref[2]
    slots, width, order = turned_ref.shape
    for slot in range(slots):
        for part, ref in enumerate((turned_ref, other_ref)):
            high, low = split(ref[slot])
            left_ref[0, slot, part * width : (part + 1) * width] = high
            left_ref[1, slot, part * width : (part + 1) * width] = low

    def term(slot, right):
        return times((left_ref[0, slot], left_ref[1, slot]), right)

    far = term(2 * h, first_ref[...])
    middle = term(1, mid_ref[...])
    if wide_stage:
        near = term(0, head_ref[...]) + term(1, tail_ref[0]) + term(2, tail_ref[1])
        far = far + middle + term(2 - 2 * h, last_ref[...])
        eye = lax.broadcasted_iota(jnp.int32, (width, width), 0) == lax.broadcasted_iota(
            jnp.int32, (width, width), 1
        )
        out_ref[0] = near[:width] + jnp.where(eye, diag_ref[...], 0.0)
    else:
        near = term(2 * (y // 2), own_ref[...]) + jnp.where(y < 2, middle, 0.0)
        far = far + jnp.where(y < 2, 0.0, middle)
        out_ref[0] = near[:width]
    out_ref[1] = near[width:]
    out_ref[2] = far[:width]
    out_ref[3] = far[width:]


def stage_tiles(where, rights, turned, other, diag=None):
    slots, width, order = turned.shape
    operands = [*rights, turned, other] + ([diag] if diag is not None else [])
    terms = 6 if diag is not None else 3
    return pl.pallas_call(
        stage_kernel,
        in_specs=[SCALARS] + [WHOLE] * len(operands),
        out_specs=WHOLE,
        out_shape=jax.ShapeDtypeStruct((4, width, width), jnp.float32),
        scratch_shapes=[pltpu.VMEM((2, slots, 2 * width, order), jnp.bfloat16)],
        compiler_params=pltpu.CompilerParams(vmem_limit_bytes=48 * 2**20),
        cost_estimate=pl.CostEstimate(
            flops=2 * 3 * terms * order * width * 2 * width,
            bytes_accessed=4 * (terms + 6) * order * width,
            transcendentals=0,
        ),
        name="stage",
    )(where, *operands)


def body(kkt, border, first_diag, assignment, panel):
    scen_index = lax.axis_index("scen")
    own_index = lax.axis_index(("row", "col"))
    zl, x = scen_index // 4, scen_index % 4
    r, y, h = own_index // 8, (own_index // 2) % 4, own_index % 2
    where = jnp.stack([r, y, h]).astype(jnp.int32)
    slots, order, width = border.shape
    first, last = 2 * h, 2 - 2 * h
    lead = 2 * (y // 2)
    diag = jnp.where(scen_index == own_index, first_diag, 0.0)[None, :]

    barrier = lax.optimization_barrier
    own_one_head = send(border[0], to_y(-1))
    own_hop = send(pick(border, 2 - lead), to_y(1))

    swapped = send(kkt, to_pair)
    ids = scen_index * slots + jnp.arange(slots, dtype=jnp.int32)
    rows = jnp.where((assignment == ids)[:, None, None], kkt, swapped)
    both = jnp.stack([rows, send(rows, to_far)])
    both, own_hop, own_one_head, middle = barrier((both, own_hop, own_one_head, border[1]))
    mine = jnp.stack([both] + [send(both, to_y(-step)) for step in (1, 2, 3)])
    far_first = send(pick(border, last), to_far)
    far_mid = send(middle, to_far)
    mine, far_first, tail, final = barrier((mine, far_first, border[1:], pick(border, first)))
    theirs = send(mine, to_core)

    own_one_tail = send(tail, to_y(-1))
    own_two = send(own_hop, to_y(1))
    far_last = send(final, to_far)
    turned = solve(where, mine, theirs, border)
    turned, far_mid, own_two, own_one_tail = barrier((turned, far_mid, own_two, own_one_tail))
    other = send(turned, to_core)
    far_two = send(send(far_first, to_y(1)), to_y(1))
    far_pair_one = send(jnp.stack([far_first, far_mid]), to_y(-1))
    shared_two = send(jnp.where(y < 2, far_mid, tail[0]), to_y(2))

    corner = corner_tiles(where, border, far_first, far_mid, turned, diag)
    corner = halve(corner, x % 2, flip_x(1))
    corner, far_last = barrier((corner, far_last))
    corner = halve(corner, x // 2, flip_x(2))
    corner, far_two, far_pair_one, other = barrier((corner, far_two, far_pair_one, other))
    far_last_one = send(far_last, to_y(-1))
    zero_stage = stage_tiles(
        where, (border[0], tail, far_first, far_mid, far_last), turned, other, diag
    )
    corner = halve(corner, zl % 2, flip_z(1))
    corner = halve(corner, zl // 2, flip_z(2))
    corner = jnp.stack([corner, send(corner, to_far)])
    corner, shared_two, far_last_one = barrier((corner, shared_two, far_last_one))
    two_stage = stage_tiles(where, (own_two, far_two, shared_two), turned, other)
    corner = double(corner, zl // 2, flip_z(2))
    corner = double(corner, zl % 2, flip_z(1))
    corner, zero_stage, two_stage = barrier((corner, zero_stage, two_stage))
    corner = double(corner, x // 2, flip_x(2))
    corner = double(corner, x % 2, flip_x(1))

    stages = jnp.stack(
        [
            zero_stage,
            stage_tiles(
                where,
                (own_one_head, own_one_tail, far_pair_one[0], far_pair_one[1], far_last_one),
                turned,
                other,
                jnp.zeros_like(diag),
            ),
            two_stage,
        ]
    )
    corner, stages = lax.optimization_barrier((corner, stages))
    inverse_cols = factor_inverse(where, corner)

    total = pick(stages, jnp.minimum(x, 2))
    got = [
        send(pick(stages, jnp.minimum((x + step) % 4, 2)), to_stage_owner(step))
        for step in (1, 2, 3)
    ]
    got, inverse_cols = lax.optimization_barrier((got, inverse_cols))
    total = reduce_pieces(total + got[0] + got[1] + got[2], zl, to_z)
    direct = send(total, final_target(False))
    mirrored = send(total, final_target(True))
    schur = direct + mirrored.T

    share = 2 * width // 16
    term = lax.dot_general(
        inverse_cols, schur, (((1,), (1,)), ((), ())), precision=HIGHEST,
        preferred_element_type=jnp.float32,
    )
    term = jnp.where(own_index // 2 == panel[0], term, 0.0).reshape(16, share, width)
    shares = lax.all_to_all(term, ("row", "col"), 0, 0, tiled=True)
    chosen = lax.dynamic_slice_in_dim(shares, 2 * panel[0], 2, 0)
    return (schur, (chosen[0] + chosen[1]).T)


def solution(mesh):
    in_specs = (
        P("scen", ("row", "col"), None),
        P("scen", None, ("row", "col")),
        P("scen"),
        P("scen"),
        P(),
    )
    out_specs = (P("scen", ("row", "col")), P("scen", ("row", "col")))
    return jax.shard_map(body, mesh=mesh, in_specs=in_specs, out_specs=out_specs, check_vma=False)
```
